32 devices in a mesh: grp: 2 (over y), pts: 4 (over z), sub: 4 (over x, core).
Axes of the slice: x: 2, y: 2, z: 4, core: 2. Of those that a mesh axis runs over, the one named last changes fastest.
Arguments:
- features: bfloat16 [8192, 256], P(('grp', 'pts', 'sub')), parts along dimension 0, may hold values from -6 to 6
- tree_order: int32 [32, 256], P(('grp', 'pts', 'sub')), parts along dimension 0, may hold values from 0 to 255, each once within a row
- rot_source: int32 [8192], P(('grp', 'pts', 'sub')), parts along dimension 0, may hold values from 0 to 4095, as said below
- rot_target: int32 [8192], P(('grp', 'pts', 'sub')), parts along dimension 0, may hold values from 0 to 4095, as said below
- counts: int32 [32], P('grp'), parts along dimension 0, may hold values from 128 to 256, as said below
- fine_gain: float32 [3, 256], replicated, may hold values from 0.1 to 1.9
- fine_qkv: bfloat16 [3, 256, 768], replicated, may hold values from -10 to 10
- fine_out: bfloat16 [3, 256, 256], replicated, may hold values from -0.375 to 0.375
- pool_weight: bfloat16 [4096, 512], replicated, may hold values from -0.09375 to 0.09375
- coarse_gain: float32 [512], replicated, may hold values from 0.1 to 1.9
- coarse_qkv: bfloat16 [512, 1536], replicated, may hold values from -10 to 10
- coarse_out: bfloat16 [512, 512], replicated, may hold values from -0.25 to 0.25
- unpool_weight: bfloat16 [512, 4096], replicated, may hold values from -0.25 to 0.25
Outputs:
- refined: bfloat16 [8192, 256], P(('grp', 'pts', 'sub')), parts along dimension 0
The draws below stay inside these ranges and needn't reach their ends.
There are 2 independent parts, one for each index of `grp`. The reference program is written for one: setup_inputs(seed, part) draws one part's arguments, and reference() takes and returns one part's arrays. A program takes and returns all parts, laid end to end along the dimension named above; an argument that names none is the same for every part. Nothing has to cross between parts.
Inputs may be any that keep to these rules, and one draw needn't show every extreme that they name: `rot_source`: A permutation of the points. The number of rotated slots of a receiving device that hold points of a sending device (itself included) depends only on k = (the receiver's flat index - the sender's) modulo 16; it is at most 24, some pairs reach 24. `rot_target`: the inverse permutation of rot_source. `counts`: multiples of 16; both ends of the range are reached.
All inputs are finite; a program needn't handle non-finite values.
Results may differ from the reference program's by a relative error of at most 0.017.
Values may be sent and summed in bfloat16 or wider, within the bound.
A program may use at most 64 MiB of HBM per device.

```python
import math
import jax
import jax.numpy as jnp
from jax import lax

WIDTH = 256
HEADS_FINE = 8
HEAD_FINE = 32
BALL = 256
STRIDE = 16
COARSE = 512
HEADS_COARSE = 8
HEAD_COARSE = 64
LAYERS = 3
NEAR = 16
PTS_DEV = 256
DEV_PART = 16
POINTS = 4096
TOKENS = 256
FAR = 4
NEAR_LOAD = 16


def shuffled_rows(key, row_count, length):
    keys = jax.random.split(key, row_count)
    return jax.vmap(lambda single: jax.random.permutation(single, length))(keys).astype(jnp.int32)


def rotation_tables(key):
    first_key, second_key, third_key = jax.random.split(key, 3)
    template = jnp.where(jnp.arange(NEAR) % 2 == 0, NEAR_LOAD + NEAR_LOAD // 2, NEAR_LOAD - NEAR_LOAD // 2).astype(jnp.int32)
    near_sizes = template[jax.random.permutation(first_key, NEAR)]
    offset_ids = jnp.arange(DEV_PART, dtype=jnp.int32)
    near_rank = (offset_ids + NEAR // 2) % DEV_PART
    block_sizes = jnp.where(near_rank < NEAR, near_sizes[jnp.minimum(near_rank, NEAR - 1)], FAR).astype(jnp.int32)
    starts = jnp.cumsum(block_sizes) - block_sizes
    slot_ids = jnp.arange(PTS_DEV, dtype=jnp.int32)
    offset = jnp.sum((starts[None, :] <= slot_ids[:, None]).astype(jnp.int32), axis=1) - 1
    shuffle = shuffled_rows(second_key, DEV_PART, PTS_DEV)
    placing = shuffled_rows(third_key, DEV_PART, PTS_DEV)
    receiver = jnp.arange(DEV_PART, dtype=jnp.int32)[:, None]
    sender = (receiver - offset[None, :]) % DEV_PART
    canonical = sender * PTS_DEV + shuffle[sender, slot_ids[None, :]]
    source = jnp.take_along_axis(canonical, placing, axis=1).reshape(-1).astype(jnp.int32)
    target = jnp.zeros((POINTS,), jnp.int32).at[source].set(jnp.arange(POINTS, dtype=jnp.int32))
    return (source, target)


def aligned_projection(key, layers, feat_width, heads, scale_top, strong, weak):
    keys = jax.random.split(key, 5)
    shape_three = (layers, feat_width, feat_width)
    base_scale = feat_width ** (-0.5)
    w_query = jax.random.normal(keys[0], shape_three, jnp.float32) * base_scale
    w_key = jax.random.normal(keys[1], shape_three, jnp.float32) * base_scale
    w_value = jax.random.normal(keys[2], shape_three, jnp.float32) * base_scale
    head_scale = jnp.exp(jax.random.uniform(keys[3], (layers, heads), jnp.float32, 0.0, math.log(scale_top)))
    picking = jax.random.uniform(keys[4], (layers, heads), jnp.float32)
    head_factor = jnp.where(picking < 0.5, strong, weak)
    column_scale = jnp.repeat(head_scale, feat_width // heads, axis=1)[:, None, :]
    column_factor = jnp.repeat(head_factor, feat_width // heads, axis=1)[:, None, :]
    w_query = jnp.clip((w_query + column_factor * w_key) * column_scale, -10.0, 10.0)
    return jnp.concatenate([w_query, w_key, w_value], axis=-1).astype(jnp.bfloat16)


def draw_rot_source(key, part):
    tables = rotation_tables(key)
    return tables[0]


def draw_rot_target(key, part):
    tables = rotation_tables(key)
    return tables[1]


def draw_counts(key, part):
    key = jax.random.fold_in(key, 11)
    first_key, second_key = jax.random.split(key)
    levels = 16 * jax.random.randint(first_key, (DEV_PART,), PTS_DEV // 32, PTS_DEV // 16 + 1)
    placing = jax.random.permutation(second_key, DEV_PART)
    levels = levels.at[placing[0]].set(PTS_DEV).at[placing[1]].set(PTS_DEV // 2)
    return levels.astype(jnp.int32)


def draw_fine_qkv(key, part):
    key = jax.random.fold_in(key, 5)
    strong = 0.0
    weak = 0.0
    return aligned_projection(key, LAYERS, WIDTH, HEADS_FINE, 1.0, strong, weak)


def draw_coarse_qkv(key, part):
    key = jax.random.fold_in(key, 7)
    strong = 0.0
    weak = 0.0
    return aligned_projection(key, 1, COARSE, HEADS_COARSE, 2.5, strong, weak)[0]


def block_levels(key, dims, cuts, low, largest):
    factor_of = 1.0
    for axis_at, blocks in cuts:
        heights = jax.random.uniform(jax.random.fold_in(jax.random.fold_in(key, 6), axis_at), (blocks,), jnp.float32, low / len(cuts), largest / len(cuts))
        factor_of = factor_of * jnp.repeat(jnp.exp(heights), dims[axis_at] // blocks).reshape((-1,) + (1,) * (len(dims) - 1 - axis_at))
    return factor_of


def noise(rng, dims, scale, most, shards=(), kind=jnp.bfloat16):
    values = jax.random.normal(rng, dims, jnp.float32) * scale
    if len(shards) > 0:
        values = block_levels(rng, dims, shards, -0.22, 0.18) * values
    return jnp.clip(values, min=-most, max=most).astype(kind)


def setup_inputs(seed: int = 0, part: int = 0) -> dict:
    splits = jax.random.split(jax.random.key(seed), 14)
    part_keys = jax.random.split(jax.random.fold_in(splits[13], part), 14)
    return {
        "features": noise(part_keys[0], (POINTS, WIDTH), 1.0, 6.0, ((0, 16),)),
        "tree_order": jax.vmap(lambda own: jax.random.permutation(own, PTS_DEV))(jax.random.split(part_keys[1], DEV_PART)).reshape((DEV_PART, PTS_DEV)).astype(jnp.int32),
        "rot_source": draw_rot_source(jax.random.fold_in(jax.random.fold_in(splits[13], part), 71), part),
        "rot_target": draw_rot_target(jax.random.fold_in(jax.random.fold_in(splits[13], part), 71), part),
        "counts": draw_counts(jax.random.fold_in(jax.random.fold_in(splits[13], part), 71), part),
        "fine_gain": jnp.clip(1.0 + 0.18 * jax.random.normal(splits[5], (LAYERS, WIDTH), jnp.float32), 0.1, 1.9),
        "fine_qkv": draw_fine_qkv(jax.random.fold_in(splits[13], 71), part),
        "fine_out": noise(splits[7], (LAYERS, WIDTH, WIDTH), WIDTH ** -0.5, 0.375),
        "pool_weight": noise(splits[8], (STRIDE * WIDTH, COARSE), (STRIDE * WIDTH) ** -0.5, 0.09375),
        "coarse_gain": jnp.clip(1.0 + 0.18 * jax.random.normal(splits[9], (COARSE,), jnp.float32), 0.1, 1.9),
        "coarse_qkv": draw_coarse_qkv(jax.random.fold_in(splits[13], 71), part),
        "coarse_out": noise(splits[11], (COARSE, COARSE), COARSE ** -0.5, 0.25),
        "unpool_weight": noise(splits[12], (COARSE, STRIDE * WIDTH), COARSE ** -0.5, 0.25),
    }


def rms_normed(values, norm_gain):
    widened = values.astype(jnp.float32)
    spread = lax.rsqrt(lax.optimization_barrier(jnp.mean(widened * widened, axis=-1, keepdims=True)) + 1e-06)
    return (widened * spread * norm_gain.astype(jnp.float32)).astype(jnp.bfloat16)

def ball_block(points, usable, norm_gain, w_packed, w_out):
    row_count, feat_width = points.shape
    ball_count = row_count // BALL
    packed = jnp.dot(rms_normed(points, norm_gain), w_packed, preferred_element_type=jnp.float32).astype(jnp.bfloat16)
    layout = (ball_count, BALL, HEADS_FINE, HEAD_FINE)
    queries = packed[:, :feat_width].reshape(layout).astype(jnp.float32)
    key_rows = packed[:, feat_width:2 * feat_width].reshape(layout).astype(jnp.float32)
    value_rows = packed[:, 2 * feat_width:].reshape(layout).astype(jnp.float32)
    scores = jnp.einsum('bqhd,bkhd->bhqk', queries, key_rows) * HEAD_FINE ** (-0.5)
    allowed = usable.reshape(ball_count, 1, 1, BALL) | jnp.eye(BALL, dtype=jnp.bool_)[None, None]
    row_peak = lax.optimization_barrier(jnp.max(jnp.where(allowed, scores, -1e+30), axis=-1, keepdims=True))
    exponent = jnp.where(allowed, jnp.exp(scores - row_peak), 0.0)
    row_total = lax.optimization_barrier(jnp.sum(exponent, axis=-1))
    weights = lax.optimization_barrier(exponent.astype(jnp.bfloat16)).astype(jnp.float32)
    mixed_heads = jnp.einsum('bhqk,bkhd->bqhd', weights, value_rows) / jnp.transpose(row_total, (0, 2, 1))[..., None]
    attended = mixed_heads.astype(jnp.bfloat16).reshape(row_count, feat_width)
    return (points.astype(jnp.float32) + jnp.dot(attended, w_out, preferred_element_type=jnp.float32)).astype(jnp.bfloat16)

def coarse_block(tokens, usable, norm_gain, w_packed, w_out):
    token_count, feat_width = tokens.shape
    packed = jnp.dot(rms_normed(tokens, norm_gain), w_packed, preferred_element_type=jnp.float32).astype(jnp.bfloat16)
    layout = (token_count, HEADS_COARSE, HEAD_COARSE)
    queries = packed[:, :feat_width].reshape(layout).astype(jnp.float32)
    key_rows = packed[:, feat_width:2 * feat_width].reshape(layout).astype(jnp.float32)
    value_rows = packed[:, 2 * feat_width:].reshape(layout).astype(jnp.float32)
    block_rows = math.gcd(512, token_count)
    token_index = jnp.arange(token_count, dtype=jnp.int32)

    def attend(first_row):
        query_block = lax.dynamic_slice_in_dim(queries, first_row, block_rows, 0)
        query_ids = lax.dynamic_slice_in_dim(token_index, first_row, block_rows, 0)
        scores = jnp.einsum('qhd,khd->hqk', query_block, key_rows) * HEAD_COARSE ** (-0.5)
        allowed = (usable[None, :] | (query_ids[:, None] == token_index[None, :]))[None]
        row_peak = lax.optimization_barrier(jnp.max(jnp.where(allowed, scores, -1e+30), axis=-1, keepdims=True))
        exponent = jnp.where(allowed, jnp.exp(scores - row_peak), 0.0)
        row_total = lax.optimization_barrier(jnp.sum(exponent, axis=-1))
        weights = lax.optimization_barrier(exponent.astype(jnp.bfloat16)).astype(jnp.float32)
        mixed_heads = jnp.einsum('hqk,khd->qhd', weights, value_rows) / jnp.transpose(row_total)[..., None]
        return mixed_heads.astype(jnp.bfloat16)
    starts = jnp.arange(token_count // block_rows, dtype=jnp.int32) * block_rows
    attended = lax.map(attend, starts).reshape(token_count, feat_width)
    return (tokens.astype(jnp.float32) + jnp.dot(attended, w_out, preferred_element_type=jnp.float32)).astype(jnp.bfloat16)

def device_blocks(points, valid_mask, layer, fine_gain, fine_qkv, fine_out):

    def one_device(pair):
        return ball_block(pair[0], pair[1], fine_gain[layer], fine_qkv[layer], fine_out[layer])
    return lax.map(one_device, (points, valid_mask))

def reference(features, tree_order, rot_source, rot_target, counts, fine_gain, fine_qkv, fine_out, pool_weight, coarse_gain, coarse_qkv, coarse_out, unpool_weight):
    blocks = features.reshape(DEV_PART, PTS_DEV, WIDTH)
    ordered = jnp.take_along_axis(blocks, tree_order[:, :, None], axis=1)
    valid_mask = jnp.arange(PTS_DEV, dtype=jnp.int32)[None, :] < counts[:, None]
    after_first = device_blocks(ordered, valid_mask, 0, fine_gain, fine_qkv, fine_out)
    flat_valid = valid_mask.reshape(POINTS)
    rotated = after_first.reshape(POINTS, WIDTH)[rot_source].reshape(DEV_PART, PTS_DEV, WIDTH)
    rotated_valid = flat_valid[rot_source].reshape(DEV_PART, PTS_DEV)
    after_rotated = device_blocks(rotated, rotated_valid, 1, fine_gain, fine_qkv, fine_out)
    restored = after_rotated.reshape(POINTS, WIDTH)[rot_target]
    masked = jnp.where(flat_valid[:, None], restored, jnp.zeros_like(restored)).reshape(TOKENS, STRIDE * WIDTH)
    coarse_tokens = jnp.dot(masked, pool_weight, preferred_element_type=jnp.float32).astype(jnp.bfloat16)
    token_valid = flat_valid.reshape(TOKENS, STRIDE)[:, 0]
    mixed_tokens = coarse_block(coarse_tokens, token_valid, coarse_gain, coarse_qkv, coarse_out)
    upsampled = jnp.dot(mixed_tokens, unpool_weight, preferred_element_type=jnp.float32).reshape(POINTS, WIDTH)
    after_unpool = (restored.astype(jnp.float32) + upsampled).astype(jnp.bfloat16)
    after_last = device_blocks(after_unpool.reshape(DEV_PART, PTS_DEV, WIDTH), valid_mask, 2, fine_gain, fine_qkv, fine_out)
    refined = jnp.where(valid_mask[:, :, None], after_last, jnp.zeros_like(after_last))
    return refined.reshape(POINTS, WIDTH)
```

```python
import functools

import jax
import jax.numpy as jnp
from jax import lax
from jax.experimental import pallas as pl
from jax.experimental.pallas import tpu as pltpu
from jax.sharding import PartitionSpec as P

HEADS_FINE = 8
HEAD_FINE = 32
HEADS_COARSE = 8
HEAD_COARSE = 64
STRIDE = 16
NEAR = 16
LOG2E = 1.4426950408889634
MESH = pl.DeviceIdType.MESH
F32 = jnp.float32
BF16 = jnp.bfloat16

NN = (((1,), (0,)), ((), ()))
NT = (((1,), (1,)), ((), ()))
TN = (((0,), (0,)), ((), ()))


def mm(a, b, dims=NN):
    return lax.dot_general(a, b, dims, preferred_element_type=F32)


def sub_iota(rows, cols):
    return lax.broadcasted_iota(jnp.int32, (rows, cols), 0)


def lane_iota(rows, cols):
    return lax.broadcasted_iota(jnp.int32, (rows, cols), 1)


def one_hot(condition):
    return jnp.where(condition, 1.0, 0.0).astype(BF16)


def normed_rows(widened, gain):
    spread = lax.rsqrt(jnp.mean(widened * widened, axis=1, keepdims=True) + 1e-6)
    return (widened * spread * gain).astype(BF16)


def ball_block(x, usable_col, gain, w_packed, w_out):
    rows, width = x.shape
    xf = x.astype(F32)
    packed = mm(normed_rows(xf, gain), w_packed).astype(BF16)
    q, k, v = packed[:, :width], packed[:, width : 2 * width], packed[:, 2 * width :]
    v_t = v.T
    allowed = usable_col | (sub_iota(rows, rows) == lane_iota(rows, rows))
    bias = jnp.where(allowed, 0.0, -1e30)
    head_of = lane_iota(1, width) // HEAD_FINE
    factor = HEAD_FINE**-0.5 * LOG2E
    heads = []
    for h in range(HEADS_FINE):
        s = mm(k * one_hot(head_of == h), q, NT) + bias
        peak = jnp.max(s, axis=0, keepdims=True)
        p = jnp.exp2((s - peak) * factor)
        total = jnp.sum(p, axis=0, keepdims=True)
        part = mm(v_t[h * HEAD_FINE : (h + 1) * HEAD_FINE, :], p.astype(BF16))
        heads.append((part / total).astype(BF16))
    attended_t = jnp.concatenate(heads, axis=0)
    return (xf + mm(attended_t, w_out, TN)).astype(BF16)


def kernel(
    n, nsub, cap,
    feat, tree, src, tgt, cnt, fgain, cgain,
    fqkv_h, fout_h, pool_h, cqkv_h, cout_h, unpool_h,
    out,
    fqkv, fout, pool, cqkv, cout, unpool,
    send_a, recv_a, send_b, recv_b, toks,
    wsem, ssem_a, rsem_a, ssem_b, rsem_b, ssem_c, rsem_c,
):
    rows, width = feat.shape
    tok = rows // STRIDE
    coarse = cqkv.shape[0]
    slots = n * cap
    me = lax.axis_index("pts") * nsub + lax.axis_index("sub")

    def peer_id(k):
        p = lax.rem(me + k + n, n)
        return {"pts": p // nsub, "sub": lax.rem(p, nsub)}

    def peers(body):
        if n <= 16:
            for k in range(1, n):
                body(k)
        else:
            def step(k, carry):
                body(k)
                return carry

            lax.fori_loop(1, n, step, 0)

    loads = [
        pltpu.make_async_copy(fqkv_h, fqkv, wsem.at[0]),
        pltpu.make_async_copy(fout_h, fout, wsem.at[1]),
        pltpu.make_async_copy(pool_h, pool, wsem.at[2]),
        pltpu.make_async_copy(cqkv_h, cqkv, wsem.at[3]),
        pltpu.make_async_copy(cout_h, cout, wsem.at[4]),
        pltpu.make_async_copy(unpool_h, unpool, wsem.at[5]),
    ]
    for load in loads:
        load.start()

    barrier = pltpu.get_barrier_semaphore()
    peers(lambda k: pl.semaphore_signal(barrier, inc=1, device_id=peer_id(k), device_id_type=MESH))

    sub_sq, lane_sq = sub_iota(rows, rows), lane_iota(rows, rows)
    shift = rows.bit_length() - 1
    tgt_hi = lax.shift_right_logical(tgt[...], shift)
    src_hi = lax.shift_right_logical(src[...], shift)
    listed = sub_iota(16, rows)
    stacked = jnp.where(listed == 0, tree[...], 0)
    stacked = jnp.where(listed == 1, tgt_hi, stacked)
    stacked = jnp.where(listed == 2, tgt[...] - tgt_hi * rows, stacked)
    stacked = jnp.where(listed == 3, src_hi, stacked)
    stacked = jnp.where(listed == 4, src[...] - src_hi * rows, stacked)
    table = stacked.astype(F32).astype(BF16)
    swap = one_hot(lane_sq == lax.rem(sub_sq, tok) * STRIDE + sub_sq // tok)
    perm_rows = mm(table, swap).astype(jnp.int32)
    perm_cols = mm(swap, table, NT).astype(jnp.int32)
    flat_cols = mm(one_hot(sub_sq == lane_sq), table, NT).astype(jnp.int32)
    my_count = jnp.sum(jnp.where(lane_iota(1, n) == me, cnt[...], 0), axis=1, keepdims=True)
    sub_col = sub_iota(rows, 1)
    usable = lax.rem(sub_col, tok) * STRIDE + sub_col // tok < my_count

    ordered = mm(one_hot(perm_cols[:, 0:1] == lane_sq), feat[...]).astype(BF16)
    loads[0].wait()
    loads[1].wait()
    after_first = ball_block(ordered, usable, fgain[0:1, :], fqkv[0], fout[0])

    def wrapped(offset):
        return jnp.where(offset < 0, offset + n, offset)

    hi_r, lo_r = perm_rows[1:2, :], perm_rows[2:3, :]
    hi_c, lo_c = perm_cols[:, 1:2], perm_cols[:, 2:3]
    same = hi_c == hi_r
    rank_r = jnp.sum(jnp.where(same & (lo_c < lo_r), 1, 0), axis=0, keepdims=True)
    slot_r = wrapped(hi_r - me) * cap + rank_r
    send_table = one_hot(sub_iota(slots, rows) == slot_r)
    outgoing = mm(send_table, after_first).astype(BF16).reshape(n, cap, width)
    send_a[...] = outgoing
    pl.semaphore_wait(barrier, n - 1)

    def copy_a(k):
        return pltpu.make_async_remote_copy(
            send_a.at[k], recv_a.at[k], ssem_a.at[k], rsem_a.at[k],
            device_id=peer_id(k), device_id_type=MESH,
        )

    peers(lambda k: copy_a(k).start())
    recv_a[0] = send_a[0]

    rank_c = jnp.sum(jnp.where(same & (lo_r < lo_c), 1, 0), axis=1, keepdims=True)
    slot_c = wrapped(hi_c - me) * cap + rank_c
    send_pick = one_hot(slot_c == lane_iota(rows, slots))
    from_r, from_c = src_hi, flat_cols[:, 3:4]
    same = from_c == from_r
    rank_r = jnp.sum(jnp.where(same & (sub_sq < lane_sq), 1, 0), axis=0, keepdims=True)
    rank_c = jnp.sum(jnp.where(same & (lane_sq < sub_sq), 1, 0), axis=1, keepdims=True)
    recv_table = one_hot(sub_iota(slots, rows) == wrapped(me - from_r) * cap + rank_r)
    recv_pick = one_hot(wrapped(me - from_c) * cap + rank_c == lane_iota(rows, slots))
    source_count = jnp.sum(
        jnp.where(from_c == lane_iota(rows, n), cnt[...], 0), axis=1, keepdims=True
    )
    usable_rot = flat_cols[:, 4:5] < source_count

    peers(lambda k: copy_a(k).wait_recv())
    rotated = mm(recv_pick, recv_a[...].reshape(slots, width)).astype(BF16)
    after_rotated = ball_block(rotated, usable_rot, fgain[1:2, :], fqkv[1], fout[1])
    send_b[...] = mm(recv_table, after_rotated).astype(BF16).reshape(n, cap, width)

    def copy_b(k):
        return pltpu.make_async_remote_copy(
            send_b.at[k], recv_b.at[k], ssem_b.at[k], rsem_b.at[k],
            device_id=peer_id(-k), device_id_type=MESH,
        )

    peers(lambda k: copy_b(k).start())
    recv_b[0] = send_b[0]
    for load in loads[2:]:
        load.wait()
    peers(lambda k: copy_b(k).wait_recv())
    restored = mm(send_pick, recv_b[...].reshape(slots, width))

    masked = jnp.where(usable, restored, 0.0).astype(BF16)
    tokens_f = jnp.zeros((tok, coarse), F32)
    for j in range(STRIDE):
        tokens_f += mm(masked[j * tok : (j + 1) * tok, :], pool[j * width : (j + 1) * width, :])
    tokens = tokens_f.astype(BF16)
    toks[me] = tokens

    def copy_c(k):
        return pltpu.make_async_remote_copy(
            toks.at[me], toks.at[me], ssem_c.at[k], rsem_c.at[k],
            device_id=peer_id(k), device_id_type=MESH,
        )

    peers(lambda k: copy_c(k).start())
    widened = tokens.astype(F32)
    q = mm(normed_rows(widened, cgain[...]), cqkv[:, :coarse]).astype(BF16)
    head_of = lane_iota(1, coarse) // HEAD_COARSE
    q_heads = jnp.concatenate([q * one_hot(head_of == h) for h in range(HEADS_COARSE)], axis=0)
    keys = n * tok
    key_count = mm(
        jnp.broadcast_to(cnt[...].astype(F32), (16, n)).astype(BF16),
        one_hot(sub_iota(n, keys) == lane_iota(n, keys) // tok),
    )[0:1, :]
    key_at = lane_iota(1, keys)
    key_valid = (lax.rem(key_at, tok) * STRIDE).astype(F32) < key_count
    stack = HEADS_COARSE * tok
    query_at = me * tok + lax.rem(sub_iota(stack, 1), tok)
    bias = jnp.where(key_valid | (query_at == key_at), 0.0, -1e30)

    peers(lambda k: copy_c(k).wait_recv())
    all_tokens = toks[...].reshape(keys, coarse)
    kv = mm(normed_rows(all_tokens.astype(F32), cgain[...]), cqkv[:, coarse:]).astype(BF16)
    s = mm(q_heads, kv[:, :coarse], NT) + bias
    peak = jnp.max(s, axis=1, keepdims=True)
    p = jnp.exp2((s - peak) * (HEAD_COARSE**-0.5 * LOG2E))
    total = jnp.sum(p, axis=1, keepdims=True)
    mixed = mm(p.astype(BF16), kv[:, coarse:]) / total
    attended = jnp.zeros((tok, coarse), F32)
    for h in range(HEADS_COARSE):
        attended += jnp.where(head_of == h, mixed[h * tok : (h + 1) * tok, :], 0.0)
    mixed_tokens = (widened + mm(attended.astype(BF16), cout[...])).astype(BF16)

    lifted = jnp.concatenate(
        [mm(mixed_tokens, unpool[:, j * width : (j + 1) * width]) for j in range(STRIDE)], axis=0
    )
    after_unpool = (restored + lifted).astype(BF16)
    after_last = ball_block(after_unpool, usable, fgain[2:3, :], fqkv[2], fout[2])
    kept = jnp.where(usable, after_last.astype(F32), 0.0).astype(BF16)
    out[...] = mm(swap, kept).astype(BF16)

    peers(lambda k: copy_a(k).wait_send())
    peers(lambda k: copy_b(k).wait_send())
    peers(lambda k: copy_c(k).wait_send())


def per_device(n, nsub, features, tree_order, rot_source, rot_target, counts, fine_gain, fine_qkv,
               fine_out, pool_weight, coarse_gain, coarse_qkv, coarse_out, unpool_weight):
    rows, width = features.shape
    coarse = coarse_gain.shape[0]
    far_load = max(1, rows // n // 4)
    near_load = (rows - far_load * (n - NEAR)) // NEAR
    cap = -(-(near_load + near_load // 2) // 16) * 16
    vmem, hbm = pl.BlockSpec(memory_space=pltpu.VMEM), pl.BlockSpec(memory_space=pl.ANY)
    weights = (fine_qkv, fine_out, pool_weight, coarse_qkv, coarse_out, unpool_weight)
    sems = pltpu.SemaphoreType.DMA((n,))
    return pl.pallas_call(
        functools.partial(kernel, n, nsub, cap),
        out_shape=jax.ShapeDtypeStruct((rows, width), BF16),
        in_specs=[vmem] * 7 + [hbm] * 6,
        out_specs=vmem,
        scratch_shapes=[pltpu.VMEM(w.shape, w.dtype) for w in weights]
        + [pltpu.VMEM((n, cap, width), BF16)] * 4
        + [pltpu.VMEM((n, rows // STRIDE, coarse), BF16)]
        + [pltpu.SemaphoreType.DMA((6,))]
        + [sems] * 6,
        compiler_params=pltpu.CompilerParams(
            collective_id=0, has_side_effects=True, vmem_limit_bytes=56 * 1024 * 1024
        ),
    )(
        features, tree_order, rot_source.reshape(1, rows), rot_target.reshape(1, rows),
        counts.reshape(1, n), fine_gain, coarse_gain.reshape(1, coarse), *weights,
    )


def solution(mesh):
    nsub = mesh.shape["sub"]
    n = mesh.shape["pts"] * nsub
    split, rows = P(("grp", "pts", "sub"), None), P(("grp", "pts", "sub"))
    return jax.shard_map(
        functools.partial(per_device, n, nsub),
        mesh=mesh,
        in_specs=(split, split, rows, rows, P("grp")) + (P(),) * 8,
        out_specs=split,
        check_vma=False,
    )
```

```python
import functools

import jax
import jax.numpy as jnp
from jax import lax
from jax.experimental import pallas as pl
from jax.experimental.pallas import tpu as pltpu
from jax.sharding import PartitionSpec as P

HEADS_FINE = 8
HEAD_FINE = 32
HEADS_COARSE = 8
HEAD_COARSE = 64
STRIDE = 16
NEAR = 16
LOG2E = 1.4426950408889634
MESH = pl.DeviceIdType.MESH
F32 = jnp.float32
BF16 = jnp.bfloat16

NN = (((1,), (0,)), ((), ()))
NT = (((1,), (1,)), ((), ()))
TN = (((0,), (0,)), ((), ()))


def mm(a, b, dims=NN):
    return lax.dot_general(a, b, dims, preferred_element_type=F32)


def sub_iota(rows, cols):
    return lax.broadcasted_iota(jnp.int32, (rows, cols), 0)


def lane_iota(rows, cols):
    return lax.broadcasted_iota(jnp.int32, (rows, cols), 1)


def div(a, b):
    return lax.shift_right_logical(a, b.bit_length() - 1) if b & (b - 1) == 0 else a // b


def mod(a, b):
    return a & (b - 1) if b & (b - 1) == 0 else lax.rem(a, b)


def one_hot(condition):
    return jnp.where(condition, 1.0, 0.0).astype(BF16)


def normed_rows(widened, gain):
    spread = lax.rsqrt(jnp.mean(widened * widened, axis=1, keepdims=True) + 1e-6)
    return (widened * spread * gain).astype(BF16)


def ball_block(x, usable_col, gain, w_packed, w_out):
    rows, width = x.shape
    xf = x.astype(F32)
    packed = mm(normed_rows(xf, gain), w_packed).astype(BF16)
    q, k, v = packed[:, :width], packed[:, width : 2 * width], packed[:, 2 * width :]
    v_t = v.T
    allowed = usable_col | (sub_iota(rows, rows) == lane_iota(rows, rows))
    bias = jnp.where(allowed, 0.0, -1e30)
    head_of = div(lane_iota(1, width), HEAD_FINE)
    factor = HEAD_FINE**-0.5 * LOG2E
    scores = []
    for h in range(0, HEADS_FINE, 2):
        pair = jnp.concatenate([k * one_hot(head_of == h), k * one_hot(head_of == h + 1)], axis=0)
        both = mm(pair, q, NT)
        scores += [both[:rows], both[rows:]]
    heads = []
    for h in range(HEADS_FINE):
        s = scores[h] + bias
        peak = jnp.max(s, axis=0, keepdims=True)
        p = jnp.exp2((s - peak) * factor)
        total = jnp.sum(p, axis=0, keepdims=True)
        part = mm(v_t[h * HEAD_FINE : (h + 1) * HEAD_FINE, :], p.astype(BF16))
        heads.append((part * (1.0 / total)).astype(BF16))
    attended_t = jnp.concatenate(heads, axis=0)
    return (xf + mm(attended_t, w_out, TN)).astype(BF16)


def slot_tables(offset, rank, at, full, half):
    tables = []
    for f in range(full):
        inside = (rank >= 16 * f) & (rank < 16 * f + 16)
        tables.append(one_hot(at == jnp.where(inside, offset * 16 + rank - 16 * f, -1)))
    if half:
        for start in (0, 8):
            slot = offset * 16 + rank - 16 * full + start
            tables.append(one_hot(at == jnp.where(rank >= 16 * full, slot, -1)))
    return tables


def pack(buffer, tables, x, full, half):
    n, _, _ = buffer.shape
    width = x.shape[1]
    for f in range(full):
        buffer[:, :, f * width : (f + 1) * width] = (
            mm(tables[f], x).astype(BF16).reshape(n, 16, width)
        )
    if half:
        mid = width // 2
        rest = mm(tables[full], x[:, :mid]) + mm(tables[full + 1], x[:, mid:])
        buffer[:, :, full * width :] = rest.astype(BF16).reshape(n, 16, mid)


def unpack(buffer, picks, width, full, half):
    n = buffer.shape[0]
    x = None
    for f in range(full):
        part = mm(picks[f], buffer[:, :, f * width : (f + 1) * width].reshape(n * 16, width))
        x = part if x is None else x + part
    if half:
        rest = buffer[:, :, full * width :].reshape(n * 16, width // 2)
        part = jnp.concatenate([mm(picks[full], rest), mm(picks[full + 1], rest)], axis=1)
        x = part if x is None else x + part
    return x


def kernel(
    n, nsub, full, half,
    feat, tree, src, tgt, cnt, fgain, cgain,
    fqkv_h, fout_h, pool_h, cqkv_h, cout_h, unpool_h,
    out,
    fqkv, fout, pool, cqkv, cout, unpool,
    send_a, recv_a, send_b, recv_b, toks,
    wsem, ssem_a, rsem_a, ssem_b, rsem_b, ssem_c, rsem_c,
):
    rows, width = feat.shape
    tok = rows // STRIDE
    coarse = cqkv.shape[0]
    slots = n * 16
    me = lax.axis_index("pts") * nsub + lax.axis_index("sub")

    def peer_id(k):
        p = mod(me + k + n, n)
        return {"pts": div(p, nsub), "sub": mod(p, nsub)}

    def peers(body):
        if n <= 16:
            for k in range(1, n):
                body(k)
        else:
            def step(k, carry):
                body(k)
                return carry

            lax.fori_loop(1, n, step, 0)

    first_loads = [
        pltpu.make_async_copy(fqkv_h.at[0], fqkv.at[0], wsem.at[0]),
        pltpu.make_async_copy(fout_h.at[0], fout.at[0], wsem.at[1]),
    ]
    later = pl.ds(1, fqkv.shape[0] - 1)
    loads = [
        pltpu.make_async_copy(fqkv_h.at[later], fqkv.at[later], wsem.at[2]),
        pltpu.make_async_copy(fout_h.at[later], fout.at[later], wsem.at[3]),
        pltpu.make_async_copy(pool_h, pool, wsem.at[4]),
        pltpu.make_async_copy(cqkv_h, cqkv, wsem.at[5]),
        pltpu.make_async_copy(cout_h, cout, wsem.at[6]),
        pltpu.make_async_copy(unpool_h, unpool, wsem.at[7]),
    ]
    for load in first_loads:
        load.start()

    barrier = pltpu.get_barrier_semaphore()
    peers(lambda k: pl.semaphore_signal(barrier, inc=1, device_id=peer_id(k), device_id_type=MESH))

    sub_sq, lane_sq = sub_iota(rows, rows), lane_iota(rows, rows)
    tgt_hi, src_hi = div(tgt[...], rows), div(src[...], rows)
    listed = sub_iota(16, rows)
    stacked = jnp.where(listed == 0, tree[...], 0)
    stacked = jnp.where(listed == 1, tgt_hi, stacked)
    stacked = jnp.where(listed == 2, tgt[...] - tgt_hi * rows, stacked)
    stacked = jnp.where(listed == 3, src_hi, stacked)
    stacked = jnp.where(listed == 4, src[...] - src_hi * rows, stacked)
    table = stacked.astype(F32).astype(BF16)
    swap = one_hot(lane_sq == mod(sub_sq, tok) * STRIDE + div(sub_sq, tok))
    perm_rows = mm(table, swap).astype(jnp.int32)
    perm_cols = mm(swap, table, NT).astype(jnp.int32)
    flat_cols = mm(one_hot(sub_sq == lane_sq), table, NT).astype(jnp.int32)
    my_count = jnp.sum(jnp.where(lane_iota(1, n) == me, cnt[...], 0), axis=1, keepdims=True)
    sub_col = sub_iota(rows, 1)
    usable = mod(sub_col, tok) * STRIDE + div(sub_col, tok) < my_count

    ordered = mm(one_hot(perm_cols[:, 0:1] == lane_sq), feat[...]).astype(BF16)
    for load in first_loads:
        load.wait()
    for load in loads:
        load.start()
    after_first = ball_block(ordered, usable, fgain[0:1, :], fqkv[0], fout[0])

    def wrapped(offset):
        return jnp.where(offset < 0, offset + n, offset)

    hi_r, lo_r = perm_rows[1:2, :], perm_rows[2:3, :]
    hi_c, lo_c = perm_cols[:, 1:2], perm_cols[:, 2:3]
    same = hi_c == hi_r
    rank_r = jnp.sum(jnp.where(same & (lo_c < lo_r), 1, 0), axis=0, keepdims=True)
    slot_down, slot_along = sub_iota(slots, rows), lane_iota(rows, slots)
    send_table = slot_tables(wrapped(hi_r - me), rank_r, slot_down, full, half)
    pack(send_a, send_table, after_first, full, half)
    pl.semaphore_wait(barrier, n - 1)

    def copy_a(k):
        return pltpu.make_async_remote_copy(
            send_a.at[k], recv_a.at[k], ssem_a.at[k], rsem_a.at[k],
            device_id=peer_id(k), device_id_type=MESH,
        )

    peers(lambda k: copy_a(k).start())
    recv_a[0] = send_a[0]

    rank_c = jnp.sum(jnp.where(same & (lo_r < lo_c), 1, 0), axis=1, keepdims=True)
    send_pick = slot_tables(wrapped(hi_c - me), rank_c, slot_along, full, half)
    from_r, from_c = src_hi, flat_cols[:, 3:4]
    same = from_c == from_r
    rank_r = jnp.sum(jnp.where(same & (sub_sq < lane_sq), 1, 0), axis=0, keepdims=True)
    rank_c = jnp.sum(jnp.where(same & (lane_sq < sub_sq), 1, 0), axis=1, keepdims=True)
    recv_table = slot_tables(wrapped(me - from_r), rank_r, slot_down, full, half)
    recv_pick = slot_tables(wrapped(me - from_c), rank_c, slot_along, full, half)
    source_count = jnp.sum(
        jnp.where(from_c == lane_iota(rows, n), cnt[...], 0), axis=1, keepdims=True
    )
    usable_rot = flat_cols[:, 4:5] < source_count

    peers(lambda k: copy_a(k).wait_recv())
    rotated = unpack(recv_a, recv_pick, width, full, half).astype(BF16)
    loads[0].wait()
    loads[1].wait()
    after_rotated = ball_block(rotated, usable_rot, fgain[1:2, :], fqkv[1], fout[1])
    pack(send_b, recv_table, after_rotated, full, half)

    def copy_b(k):
        return pltpu.make_async_remote_copy(
            send_b.at[k], recv_b.at[k], ssem_b.at[k], rsem_b.at[k],
            device_id=peer_id(-k), device_id_type=MESH,
        )

    peers(lambda k: copy_b(k).start())
    recv_b[0] = send_b[0]
    for load in loads[2:]:
        load.wait()
    peers(lambda k: copy_b(k).wait_recv())
    restored = unpack(recv_b, send_pick, width, full, half)

    masked = jnp.where(usable, restored, 0.0).astype(BF16)
    tokens_f = jnp.zeros((tok, coarse), F32)
    for j in range(STRIDE):
        tokens_f += mm(masked[j * tok : (j + 1) * tok, :], pool[j * width : (j + 1) * width, :])
    tokens = tokens_f.astype(BF16)
    toks[me] = tokens

    def copy_c(k):
        return pltpu.make_async_remote_copy(
            toks.at[me], toks.at[me], ssem_c.at[k], rsem_c.at[k],
            device_id=peer_id(k), device_id_type=MESH,
        )

    peers(lambda k: copy_c(k).start())
    widened = tokens.astype(F32)
    q = mm(normed_rows(widened, cgain[...]), cqkv[:, :coarse]).astype(BF16)
    head_of = div(lane_iota(1, coarse), HEAD_COARSE)
    q_heads = jnp.concatenate([q * one_hot(head_of == h) for h in range(HEADS_COARSE)], axis=0)
    keys = n * tok
    key_count = mm(
        jnp.broadcast_to(cnt[...].astype(F32), (16, n)).astype(BF16),
        one_hot(sub_iota(n, keys) == div(lane_iota(n, keys), tok)),
    )[0:1, :]
    key_at = lane_iota(1, keys)
    key_valid = (mod(key_at, tok) * STRIDE).astype(F32) < key_count
    stack = HEADS_COARSE * tok
    query_at = me * tok + mod(sub_iota(stack, 1), tok)
    bias = jnp.where(key_valid | (query_at == key_at), 0.0, -1e30)

    peers(lambda k: copy_c(k).wait_recv())
    all_tokens = toks[...].reshape(keys, coarse)
    kv = mm(normed_rows(all_tokens.astype(F32), cgain[...]), cqkv[:, coarse:]).astype(BF16)
    s = mm(q_heads, kv[:, :coarse], NT) + bias
    peak = jnp.max(s, axis=1, keepdims=True)
    p = jnp.exp2((s - peak) * (HEAD_COARSE**-0.5 * LOG2E))
    total = jnp.sum(p, axis=1, keepdims=True)
    mixed = mm(p.astype(BF16), kv[:, coarse:]) / total
    attended = jnp.zeros((tok, coarse), F32)
    for h in range(HEADS_COARSE):
        attended += jnp.where(head_of == h, mixed[h * tok : (h + 1) * tok, :], 0.0)
    mixed_tokens = (widened + mm(attended.astype(BF16), cout[...])).astype(BF16)

    lifted = jnp.concatenate(
        [mm(mixed_tokens, unpool[:, j * width : (j + 1) * width]) for j in range(STRIDE)], axis=0
    )
    after_unpool = (restored + lifted).astype(BF16)
    after_last = ball_block(after_unpool, usable, fgain[2:3, :], fqkv[2], fout[2])
    kept = jnp.where(usable, after_last.astype(F32), 0.0).astype(BF16)
    out[...] = mm(swap, kept).astype(BF16)

    peers(lambda k: copy_a(k).wait_send())
    peers(lambda k: copy_b(k).wait_send())
    peers(lambda k: copy_c(k).wait_send())


def per_device(n, nsub, features, tree_order, rot_source, rot_target, counts, fine_gain, fine_qkv,
               fine_out, pool_weight, coarse_gain, coarse_qkv, coarse_out, unpool_weight):
    rows, width = features.shape
    coarse = coarse_gain.shape[0]
    far_load = max(1, rows // n // 4)
    near_load = (rows - far_load * (n - NEAR)) // NEAR
    cap = near_load + near_load // 2
    full, half = cap // 16, 0 < cap % 16 <= 8
    if cap % 16 > 8:
        full += 1
    block = full * width + (width // 2 if half else 0)
    vmem, hbm = pl.BlockSpec(memory_space=pltpu.VMEM), pl.BlockSpec(memory_space=pl.ANY)
    weights = (fine_qkv, fine_out, pool_weight, coarse_qkv, coarse_out, unpool_weight)
    sems = pltpu.SemaphoreType.DMA((n,))
    return pl.pallas_call(
        functools.partial(kernel, n, nsub, full, half),
        out_shape=jax.ShapeDtypeStruct((rows, width), BF16),
        in_specs=[vmem] * 7 + [hbm] * 6,
        out_specs=vmem,
        scratch_shapes=[pltpu.VMEM(w.shape, w.dtype) for w in weights]
        + [pltpu.VMEM((n, 16, block), BF16)] * 4
        + [pltpu.VMEM((n, rows // STRIDE, coarse), BF16)]
        + [pltpu.SemaphoreType.DMA((8,))]
        + [sems] * 6,
        compiler_params=pltpu.CompilerParams(
            collective_id=0, has_side_effects=True, vmem_limit_bytes=56 * 1024 * 1024
        ),
    )(
        features, tree_order, rot_source.reshape(1, rows), rot_target.reshape(1, rows),
        counts.reshape(1, n), fine_gain, coarse_gain.reshape(1, coarse), *weights,
    )


def solution(mesh):
    nsub = mesh.shape["sub"]
    n = mesh.shape["pts"] * nsub
    split, rows = P(("grp", "pts", "sub"), None), P(("grp", "pts", "sub"))
    return jax.shard_map(
        functools.partial(per_device, n, nsub),
        mesh=mesh,
        in_specs=(split, split, rows, rows, P("grp")) + (P(),) * 8,
        out_specs=split,
        check_vma=False,
    )
```

```python
import functools

import jax
import jax.numpy as jnp
from jax import lax
from jax.experimental import pallas as pl
from jax.experimental.pallas import tpu as pltpu
from jax.sharding import PartitionSpec as P

HEADS_FINE = 8
HEAD_FINE = 32
HEADS_COARSE = 8
HEAD_COARSE = 64
STRIDE = 16
NEAR = 16
LOG2E = 1.4426950408889634
MESH = pl.DeviceIdType.MESH
F32 = jnp.float32
BF16 = jnp.bfloat16

NN = (((1,), (0,)), ((), ()))
NT = (((1,), (1,)), ((), ()))
TN = (((0,), (0,)), ((), ()))


def mm(a, b, dims=NN):
    return lax.dot_general(a, b, dims, preferred_element_type=F32)


def sub_iota(rows, cols):
    return lax.broadcasted_iota(jnp.int32, (rows, cols), 0)


def lane_iota(rows, cols):
    return lax.broadcasted_iota(jnp.int32, (rows, cols), 1)


def div(a, b):
    return lax.shift_right_logical(a, b.bit_length() - 1) if b & (b - 1) == 0 else a // b


def mod(a, b):
    return a & (b - 1) if b & (b - 1) == 0 else lax.rem(a, b)


def one_hot(condition):
    return jnp.where(condition, 1.0, 0.0).astype(BF16)


def normed_rows(widened, gain):
    spread = lax.rsqrt(jnp.mean(widened * widened, axis=1, keepdims=True) + 1e-6)
    return (widened * spread * gain).astype(BF16)


def ball_block(x, usable_col, gain, w_packed, w_out):
    rows, width = x.shape
    xf = x.astype(F32)
    packed = mm(normed_rows(xf, gain), w_packed).astype(BF16)
    q, k, v = packed[:, :width], packed[:, width : 2 * width], packed[:, 2 * width :]
    v_t = v.T
    allowed = usable_col | (sub_iota(rows, rows) == lane_iota(rows, rows))
    bias = jnp.where(allowed, 0.0, -1e30)
    head_of = div(lane_iota(1, width), HEAD_FINE)
    factor = HEAD_FINE**-0.5 * LOG2E
    scores = []
    for h in range(0, HEADS_FINE, 2):
        pair = jnp.concatenate([k * one_hot(head_of == h), k * one_hot(head_of == h + 1)], axis=0)
        both = mm(pair, q, NT)
        scores += [both[:rows], both[rows:]]
    heads = []
    for h in range(HEADS_FINE):
        s = scores[h] + bias
        peak = jnp.max(s, axis=0, keepdims=True)
        p = jnp.exp2((s - peak) * factor)
        total = jnp.sum(p, axis=0, keepdims=True)
        part = mm(v_t[h * HEAD_FINE : (h + 1) * HEAD_FINE, :], p.astype(BF16))
        heads.append((part * (1.0 / total)).astype(BF16))
    attended_t = jnp.concatenate(heads, axis=0)
    return (xf + mm(attended_t, w_out, TN)).astype(BF16)


def slot_tables(offset, rank, at, full, half):
    tables = []
    for f in range(full):
        inside = (rank >= 16 * f) & (rank < 16 * f + 16)
        tables.append(one_hot(at == jnp.where(inside, offset * 16 + rank - 16 * f, -1)))
    if half:
        for start in (0, 8):
            slot = offset * 16 + rank - 16 * full + start
            tables.append(one_hot(at == jnp.where(rank >= 16 * full, slot, -1)))
    return tables


def pack(buffer, tables, x, full, half):
    n, _, _ = buffer.shape
    width = x.shape[1]
    for f in range(full):
        buffer[:, :, f * width : (f + 1) * width] = (
            mm(tables[f], x).astype(BF16).reshape(n, 16, width)
        )
    if half:
        mid = width // 2
        rest = mm(tables[full], x[:, :mid]) + mm(tables[full + 1], x[:, mid:])
        buffer[:, :, full * width :] = rest.astype(BF16).reshape(n, 16, mid)


def unpack(buffer, picks, width, full, half):
    n = buffer.shape[0]
    x = None
    for f in range(full):
        part = mm(picks[f], buffer[:, :, f * width : (f + 1) * width].reshape(n * 16, width))
        x = part if x is None else x + part
    if half:
        rest = buffer[:, :, full * width :].reshape(n * 16, width // 2)
        part = jnp.concatenate([mm(picks[full], rest), mm(picks[full + 1], rest)], axis=1)
        x = part if x is None else x + part
    return x


def kernel(
    n, nsub, full, half,
    feat_h, tree, src, tgt, cnt, fgain, cgain,
    fqkv_h, fout_h, pool_h, cqkv_h, cout_h, unpool_h,
    out,
    feat, fqkv, fout, pool, cqkv, cout, unpool,
    send_a, recv_a, send_b, recv_b, toks,
    wsem, ssem_a, rsem_a, ssem_b, rsem_b, ssem_c, rsem_c,
):
    rows, width = feat_h.shape
    tok = rows // STRIDE
    coarse = cqkv.shape[0]
    slots = n * 16
    me = lax.axis_index("pts") * nsub + lax.axis_index("sub")

    def peer_id(k):
        p = mod(me + k + n, n)
        return {"pts": div(p, nsub), "sub": mod(p, nsub)}

    def peers(body):
        if n <= 16:
            for k in range(1, n):
                body(k)
        else:
            def step(k, carry):
                body(k)
                return carry

            lax.fori_loop(1, n, step, 0)

    first_loads = [
        pltpu.make_async_copy(fqkv_h.at[0], fqkv.at[0], wsem.at[0]),
        pltpu.make_async_copy(fout_h.at[0], fout.at[0], wsem.at[1]),
    ]
    later = pl.ds(1, fqkv.shape[0] - 1)
    loads = [
        pltpu.make_async_copy(fqkv_h.at[later], fqkv.at[later], wsem.at[2]),
        pltpu.make_async_copy(fout_h.at[later], fout.at[later], wsem.at[3]),
        pltpu.make_async_copy(pool_h, pool, wsem.at[4]),
        pltpu.make_async_copy(cqkv_h, cqkv, wsem.at[5]),
        pltpu.make_async_copy(cout_h, cout, wsem.at[6]),
        pltpu.make_async_copy(unpool_h, unpool, wsem.at[7]),
    ]
    feat_load = pltpu.make_async_copy(feat_h, feat, wsem.at[8])
    feat_load.start()
    for load in first_loads:
        load.start()

    barrier = pltpu.get_barrier_semaphore()
    peers(lambda k: pl.semaphore_signal(barrier, inc=1, device_id=peer_id(k), device_id_type=MESH))

    sub_sq, lane_sq = sub_iota(rows, rows), lane_iota(rows, rows)
    tgt_hi, src_hi = div(tgt[...], rows), div(src[...], rows)
    listed = sub_iota(16, rows)
    stacked = jnp.where(listed == 0, tree[...], 0)
    stacked = jnp.where(listed == 1, tgt_hi, stacked)
    stacked = jnp.where(listed == 2, tgt[...] - tgt_hi * rows, stacked)
    stacked = jnp.where(listed == 3, src_hi, stacked)
    stacked = jnp.where(listed == 4, src[...] - src_hi * rows, stacked)
    table = stacked.astype(F32).astype(BF16)
    swap = one_hot(lane_sq == mod(sub_sq, tok) * STRIDE + div(sub_sq, tok))
    perm_rows = mm(table, swap).astype(jnp.int32)
    perm_cols = mm(swap, table, NT).astype(jnp.int32)
    flat_cols = mm(one_hot(sub_sq == lane_sq), table, NT).astype(jnp.int32)
    my_count = jnp.sum(jnp.where(lane_iota(1, n) == me, cnt[...], 0), axis=1, keepdims=True)
    sub_col = sub_iota(rows, 1)
    usable = mod(sub_col, tok) * STRIDE + div(sub_col, tok) < my_count

    def wrapped(offset):
        return jnp.where(offset < 0, offset + n, offset)

    hi_r, lo_r = perm_rows[1:2, :], perm_rows[2:3, :]
    hi_c, lo_c = perm_cols[:, 1:2], perm_cols[:, 2:3]
    same = hi_c == hi_r
    rank_r = jnp.sum(jnp.where(same & (lo_c < lo_r), 1, 0), axis=0, keepdims=True)
    slot_down, slot_along = sub_iota(slots, rows), lane_iota(rows, slots)
    send_table = slot_tables(wrapped(hi_r - me), rank_r, slot_down, full, half)
    feat_load.wait()
    ordered = mm(one_hot(perm_cols[:, 0:1] == lane_sq), feat[...]).astype(BF16)
    for load in first_loads:
        load.wait()
    for load in loads:
        load.start()
    after_first = ball_block(ordered, usable, fgain[0:1, :], fqkv[0], fout[0])

    pack(send_a, send_table, after_first, full, half)
    pl.semaphore_wait(barrier, n - 1)

    def copy_a(k):
        return pltpu.make_async_remote_copy(
            send_a.at[k], recv_a.at[k], ssem_a.at[k], rsem_a.at[k],
            device_id=peer_id(k), device_id_type=MESH,
        )

    peers(lambda k: copy_a(k).start())
    recv_a[0] = send_a[0]

    rank_c = jnp.sum(jnp.where(same & (lo_r < lo_c), 1, 0), axis=1, keepdims=True)
    send_pick = slot_tables(wrapped(hi_c - me), rank_c, slot_along, full, half)
    from_r, from_c = src_hi, flat_cols[:, 3:4]
    same = from_c == from_r
    rank_r = jnp.sum(jnp.where(same & (sub_sq < lane_sq), 1, 0), axis=0, keepdims=True)
    rank_c = jnp.sum(jnp.where(same & (lane_sq < sub_sq), 1, 0), axis=1, keepdims=True)
    recv_table = slot_tables(wrapped(me - from_r), rank_r, slot_down, full, half)
    recv_pick = slot_tables(wrapped(me - from_c), rank_c, slot_along, full, half)
    source_count = jnp.sum(
        jnp.where(from_c == lane_iota(rows, n), cnt[...], 0), axis=1, keepdims=True
    )
    usable_rot = flat_cols[:, 4:5] < source_count

    peers(lambda k: copy_a(k).wait_recv())
    rotated = unpack(recv_a, recv_pick, width, full, half).astype(BF16)
    loads[0].wait()
    loads[1].wait()
    after_rotated = ball_block(rotated, usable_rot, fgain[1:2, :], fqkv[1], fout[1])
    pack(send_b, recv_table, after_rotated, full, half)

    def copy_b(k):
        return pltpu.make_async_remote_copy(
            send_b.at[k], recv_b.at[k], ssem_b.at[k], rsem_b.at[k],
            device_id=peer_id(-k), device_id_type=MESH,
        )

    peers(lambda k: copy_b(k).start())
    recv_b[0] = send_b[0]
    for load in loads[2:]:
        load.wait()
    peers(lambda k: copy_b(k).wait_recv())
    restored = unpack(recv_b, send_pick, width, full, half)

    masked = jnp.where(usable, restored, 0.0).astype(BF16)
    side_by_side = jnp.concatenate(
        [masked[j * tok : (j + 1) * tok, :] for j in range(STRIDE)], axis=1
    )
    tokens_f = mm(side_by_side, pool[...])
    tokens = tokens_f.astype(BF16)
    toks[me] = tokens

    def copy_c(k):
        return pltpu.make_async_remote_copy(
            toks.at[me], toks.at[me], ssem_c.at[k], rsem_c.at[k],
            device_id=peer_id(k), device_id_type=MESH,
        )

    peers(lambda k: copy_c(k).start())
    widened = tokens.astype(F32)
    q = mm(normed_rows(widened, cgain[...]), cqkv[:, :coarse]).astype(BF16)
    head_of = div(lane_iota(1, coarse), HEAD_COARSE)
    q_heads = jnp.concatenate([q * one_hot(head_of == h) for h in range(HEADS_COARSE)], axis=0)
    keys = n * tok
    key_count = mm(
        jnp.broadcast_to(cnt[...].astype(F32), (16, n)).astype(BF16),
        one_hot(sub_iota(n, keys) == div(lane_iota(n, keys), tok)),
    )[0:1, :]
    key_at = lane_iota(1, keys)
    key_valid = (mod(key_at, tok) * STRIDE).astype(F32) < key_count
    stack = HEADS_COARSE * tok
    query_at = me * tok + mod(sub_iota(stack, 1), tok)
    bias = jnp.where(key_valid | (query_at == key_at), 0.0, -1e30)

    peers(lambda k: copy_c(k).wait_recv())
    all_tokens = toks[...].reshape(keys, coarse)
    kv = mm(normed_rows(all_tokens.astype(F32), cgain[...]), cqkv[:, coarse:]).astype(BF16)
    s = mm(q_heads, kv[:, :coarse], NT) + bias
    peak = jnp.max(s, axis=1, keepdims=True)
    p = jnp.exp2((s - peak) * (HEAD_COARSE**-0.5 * LOG2E))
    total = jnp.sum(p, axis=1, keepdims=True)
    mixed = mm(p.astype(BF16), kv[:, coarse:]) / total
    attended = jnp.zeros((tok, coarse), F32)
    for h in range(HEADS_COARSE):
        attended += jnp.where(head_of == h, mixed[h * tok : (h + 1) * tok, :], 0.0)
    mixed_tokens = (widened + mm(attended.astype(BF16), cout[...])).astype(BF16)

    wide = mm(mixed_tokens, unpool[...])
    lifted = jnp.concatenate([wide[:, j * width : (j + 1) * width] for j in range(STRIDE)], axis=0)
    after_unpool = (restored + lifted).astype(BF16)
    after_last = ball_block(after_unpool, usable, fgain[2:3, :], fqkv[2], fout[2])
    kept = jnp.where(usable, after_last.astype(F32), 0.0).astype(BF16)
    out[...] = mm(swap, kept).astype(BF16)

    peers(lambda k: copy_a(k).wait_send())
    peers(lambda k: copy_b(k).wait_send())
    peers(lambda k: copy_c(k).wait_send())


def per_device(n, nsub, features, tree_order, rot_source, rot_target, counts, fine_gain, fine_qkv,
               fine_out, pool_weight, coarse_gain, coarse_qkv, coarse_out, unpool_weight):
    rows, width = features.shape
    coarse = coarse_gain.shape[0]
    far_load = max(1, rows // n // 4)
    near_load = (rows - far_load * (n - NEAR)) // NEAR
    cap = near_load + near_load // 2
    full, half = cap // 16, 0 < cap % 16 <= 8
    if cap % 16 > 8:
        full += 1
    block = full * width + (width // 2 if half else 0)
    vmem, hbm = pl.BlockSpec(memory_space=pltpu.VMEM), pl.BlockSpec(memory_space=pl.ANY)
    weights = (fine_qkv, fine_out, pool_weight, coarse_qkv, coarse_out, unpool_weight)
    sems = pltpu.SemaphoreType.DMA((n,))
    return pl.pallas_call(
        functools.partial(kernel, n, nsub, full, half),
        out_shape=jax.ShapeDtypeStruct((rows, width), BF16),
        in_specs=[hbm] + [vmem] * 6 + [hbm] * 6,
        out_specs=vmem,
        scratch_shapes=[pltpu.VMEM(features.shape, BF16)]
        + [pltpu.VMEM(w.shape, w.dtype) for w in weights]
        + [pltpu.VMEM((n, 16, block), BF16)] * 4
        + [pltpu.VMEM((n, rows // STRIDE, coarse), BF16)]
        + [pltpu.SemaphoreType.DMA((9,))]
        + [sems] * 6,
        compiler_params=pltpu.CompilerParams(
            collective_id=0, has_side_effects=True, vmem_limit_bytes=56 * 1024 * 1024
        ),
    )(
        features, tree_order, rot_source.reshape(1, rows), rot_target.reshape(1, rows),
        counts.reshape(1, n), fine_gain, coarse_gain.reshape(1, coarse), *weights,
    )


def solution(mesh):
    nsub = mesh.shape["sub"]
    n = mesh.shape["pts"] * nsub
    split, rows = P(("grp", "pts", "sub"), None), P(("grp", "pts", "sub"))
    return jax.shard_map(
        functools.partial(per_device, n, nsub),
        mesh=mesh,
        in_specs=(split, split, rows, rows, P("grp")) + (P(),) * 8,
        out_specs=split,
        check_vma=False,
    )
```
